32 devices in a mesh: blk: 16 (over z, y, core), narrow: 2 (over x).
Axes of the slice: x: 2, y: 2, z: 4, core: 2. Of those that a mesh axis runs over, the one named last changes fastest.
Arguments:
- vectors: bfloat16 [8192, 768], P(('blk', 'narrow')), may hold values from -8 to 8
- centroids: bfloat16 [65536, 768], P('blk'), may hold values from -1 to 1
- list_owner: int32 [8192, 1], P(('blk', 'narrow')), may hold values from 0 to 15; in each aligned block of 256 rows (0 to 255, 256 to 511, ...) at most 32 rows name the same one
- list_local: int32 [8192], P(('blk', 'narrow')), may hold values from 0 to 4095
Outputs:
- panel_sums: float32 [65536, 768], P(('blk', 'narrow'))
- panel_counts: float32 [65536], P(('blk', 'narrow'))
- posted: bfloat16 [16384, 768], P(('blk', 'narrow'))
The draws below stay inside these ranges and needn't reach their ends.
Inputs may be any that keep to these rules, and one draw needn't show every extreme that they name: `list_owner`: among the 256 rows of one device, at most 32 name the same owner, and in every draw some device's rows name some owner exactly 32 times.
All inputs are finite; a program needn't handle non-finite values.
Results may differ from the reference program's by a relative error of at most 0.0065.
Values may be sent and summed in bfloat16 or wider, within the bound.
A program may use at most 128 MiB of HBM per device.

```python
import math
from functools import partial
import jax
import jax.numpy as jnp
import numpy as np
from jax import lax

D = 768
PANEL = 4096
STOPS = 2
VEC_DEV = 256
CAP = 32
KCENT = 65536
SLAB = 512
VECTORS = 8192
POSTED = 16384
N_BLK = 16
N_NARROW = 2


def draw_centroids(key, part):
    inner = jax.random.fold_in(key, 21)
    result = jax.random.truncated_normal(inner, -4.0, 4.0, (KCENT, D)) / math.sqrt(D)
    return result.astype(jnp.bfloat16)


def draw_vectors(key, part):
    inner = jax.random.fold_in(key, 31)
    result = jax.random.truncated_normal(inner, -6.0, 6.0, (VECTORS, D))
    return result.astype(jnp.bfloat16)


def place_ends(entries, stream_key, smallest, high):
    extent = entries.shape
    index_at = [jax.random.randint(jax.random.fold_in(stream_key, axis), (), 0, extent[axis]) for axis in range(len(extent))]
    entries = entries.at[tuple(index_at)].set(smallest)
    longest = extent.index(max(extent))
    index_at[longest] = (index_at[longest] + 1) % extent[longest]
    return entries.at[tuple(index_at)].set(high)


def cumulative_ranks(number_of, lean):
    loads = [(1 << 20) // math.isqrt(grade ** lean) + 1 for grade in range(1, number_of + 1)]
    scale = 1 + sum(loads) // (1 << 30)
    return np.cumsum(np.array([max(1, weight // scale) for weight in loads]))


def ranked(key, extent, number_of, skew):
    table = cumulative_ranks(number_of, skew)
    lot = jax.random.randint(jax.random.fold_in(key, 1), extent, 0, int(table[number_of - 1]))
    grade = jnp.searchsorted(jnp.asarray(table, jnp.int32), lot, side="right")
    return jax.random.permutation(jax.random.fold_in(key, 2), number_of)[grade].astype(jnp.int32)


def assign_block(rng, own, number, rows, count, top, reach, skew):
    ranking = jax.random.permutation(rng, count)
    crowded, usual = load_shares(count, rows * top, reach, skew, True), load_shares(count, rows * top, reach, skew, False)
    places = jnp.arange(count)

    def named(tallies, offset_by):
        used = int((tallies > 0).sum())
        fixed = max(1, used // 4)
        passed = fixed + (places - fixed + offset_by * (used - fixed)) % max(1, count - fixed)
        return jnp.zeros((count,), jnp.int32).at[ranking[jnp.where(places < fixed, places, passed)]].set(jnp.asarray(tallies, jnp.int32))

    tallies = jnp.where(number % 4 == 0, named(crowded, number // 4), named(usual, number - number // 4 - 1))
    mixed = jax.random.permutation(jax.random.fold_in(own, 3), count)
    giver, taker = mixed[0:count // 2 * 2:2], mixed[1:count // 2 * 2:2]
    slack = jnp.minimum(tallies[giver] - 1, reach - tallies[taker]) // 2
    slack = jnp.where((giver == ranking[0]) | (taker == ranking[0]) | (tallies[taker] == 0), 0, jnp.maximum(slack, 0))
    passed = jax.random.randint(jax.random.fold_in(own, 4), (count // 2,), 0, 1 << 20) % (slack + 1)
    tallies = tallies.at[giver].add(-passed).at[taker].add(passed)
    members = jnp.searchsorted(jnp.cumsum(tallies), jnp.arange(rows * top), side="right").astype(jnp.int32)
    listing = members.reshape(top, rows).T
    listing = listing[jax.random.permutation(jax.random.fold_in(own, 1), rows)]
    offset_by = jax.random.randint(jax.random.fold_in(own, 2), (rows, 1), 0, top)
    return jnp.take_along_axis(listing, (jnp.arange(top)[None, :] + offset_by) % top, axis=1)


def load_shares(count, total, bound, lean, full):
    portions = [(1 << 20) // math.isqrt(grade ** lean) + 1 for grade in range(1, count + 1)]
    largest = bound if full else min(bound, max(-(-total // count), total * portions[0] // sum(portions)))
    least = 1 if total - largest >= count - 1 else 0
    given, spare = [largest] + [least] * (count - 1), total - largest - least * (count - 1)
    while spare > 0:
        movable = [i for i in range(1, count) if given[i] < largest] or [i for i in range(1, count) if given[i] < bound]
        mass, left = sum([portions[i] for i in movable]), spare
        for i in movable:
            addition = min(bound - given[i], max(1, left * portions[i] // mass), spare)
            given[i] = given[i] + addition
            spare = spare - addition
    return np.array(given)


def setup_inputs(seed: int = 0) -> dict:
    key_list = jax.random.split(jax.random.key(seed), 5)
    vectors = draw_vectors(jax.random.fold_in(key_list[4], 71), 0)
    centroids = draw_centroids(jax.random.fold_in(key_list[4], 71), 0)
    list_owner_keys = jax.random.split(jax.random.fold_in(key_list[2], 1), VECTORS // VEC_DEV)
    list_owner_turns = jax.random.permutation(jax.random.fold_in(key_list[2], 3), VECTORS // VEC_DEV)
    list_owner = jax.vmap(lambda own, number: assign_block(jax.random.fold_in(key_list[2], 2), own, number, VEC_DEV, N_BLK, 1, CAP, 2))(list_owner_keys, list_owner_turns).reshape((VECTORS, 1))
    list_local = place_ends(ranked(key_list[3], (VECTORS,), PANEL, 2), jax.random.fold_in(key_list[3], 3), 0, PANEL - 1).astype(jnp.int32)
    return {"vectors": vectors, "centroids": centroids, "list_owner": list_owner, "list_local": list_local}


temper = 0.5


def window_logits(row_block, panel_rows):
    norms = jnp.sum(jnp.square(panel_rows.astype(jnp.float32)), axis=1)
    product = lax.dot_general(row_block, panel_rows, (((1,), (1,)), ((), ())), preferred_element_type=jnp.float32)
    return (product - 0.5 * norms[None, :]) / temper


def post_rows(residual, owner, local, owner_count, capacity, panel_size):
    row_total = residual.shape[0]
    places = jnp.arange(row_total, dtype=jnp.int32)
    sort_key = (owner * panel_size + local) * row_total + places
    order = jnp.argsort(sort_key)
    sorted_owner = owner[order]
    owner_ids = jnp.arange(owner_count, dtype=jnp.int32)
    onehot = (owner[:, None] == owner_ids[None, :]).astype(jnp.int32)
    owner_rows = jnp.sum(onehot, axis=0).astype(jnp.int32)
    owner_start = (jnp.cumsum(owner_rows) - owner_rows).astype(jnp.int32)
    first_place = jnp.sum(jnp.where(sorted_owner[:, None] == owner_ids[None, :], owner_start[None, :], 0), axis=1).astype(jnp.int32)
    slot_index = places - first_place
    buffer = jnp.zeros((owner_count, capacity, residual.shape[1]), residual.dtype)
    return buffer.at[sorted_owner, slot_index].set(residual[order])


def reference(vectors, centroids, list_owner, list_local):
    groups = vectors.reshape(N_BLK, SLAB, D)
    owners = list_owner[:, 0].reshape(N_BLK, N_NARROW, VEC_DEV)
    local_lists = list_local.reshape(N_BLK, N_NARROW, VEC_DEV)
    group_ids = jnp.arange(N_BLK, dtype=jnp.int32)
    poster = jax.vmap(partial(post_rows, owner_count=N_BLK, capacity=CAP, panel_size=PANEL))

    def visit(carry, inputs):
        sums, counts = carry
        row_block, owner, local, group = inputs
        starts = [(((group - shift_by) % N_BLK) * PANEL).astype(jnp.int32) for shift_by in range(STOPS)]
        window = jnp.concatenate([lax.dynamic_slice_in_dim(centroids, first, PANEL, 0) for first in starts], axis=0)
        logits = window_logits(row_block, window)
        row_top = jnp.max(logits, axis=1, keepdims=True)
        log_total = row_top + jnp.log(jnp.sum(jnp.exp(logits - row_top), axis=1, keepdims=True))
        weights = jnp.exp(logits - log_total).astype(jnp.bfloat16)
        mixture = jnp.dot(weights, window, preferred_element_type=jnp.float32)
        residual = (row_block.astype(jnp.float32) - mixture).astype(jnp.bfloat16)
        split_weights = weights.reshape(N_NARROW, VEC_DEV, STOPS * PANEL).astype(jnp.float32)
        split_rows = row_block.reshape(N_NARROW, VEC_DEV, D).astype(jnp.float32)
        sum_terms = jnp.einsum("nvk,nvd->nkd", split_weights, split_rows).astype(jnp.bfloat16)
        sum_terms = jnp.sum(lax.optimization_barrier(sum_terms).astype(jnp.float32), axis=0)
        count_terms = jnp.sum(split_weights, axis=1).astype(jnp.bfloat16)
        count_terms = jnp.sum(lax.optimization_barrier(count_terms).astype(jnp.float32), axis=0)
        for shift_by in range(STOPS):
            first = starts[shift_by]
            piece = sum_terms[shift_by * PANEL:(shift_by + 1) * PANEL]
            tally = count_terms[shift_by * PANEL:(shift_by + 1) * PANEL]
            sums = lax.dynamic_update_slice_in_dim(sums, lax.dynamic_slice_in_dim(sums, first, PANEL, 0) + piece, first, 0)
            counts = lax.dynamic_update_slice_in_dim(counts, lax.dynamic_slice_in_dim(counts, first, PANEL, 0) + tally, first, 0)
        buffers = poster(residual.reshape(N_NARROW, VEC_DEV, D), owner, local)
        return (sums, counts), buffers

    start_carry = (jnp.zeros((KCENT, D), jnp.float32), jnp.zeros((KCENT,), jnp.float32))
    (panel_sums, panel_counts), buffers = lax.scan(visit, start_carry, (groups, owners, local_lists, group_ids))
    posted = jnp.transpose(buffers, (2, 1, 0, 3, 4)).reshape(POSTED, D)
    return panel_sums, panel_counts, posted
```

```python
import functools

import jax
import jax.numpy as jnp
from jax import lax
from jax.experimental import pallas as pl
from jax.experimental.pallas import tpu as pltpu
from jax.sharding import PartitionSpec as P

MESH = pl.DeviceIdType.MESH
F32 = jnp.float32
BF16 = jnp.bfloat16
EARLY = 2


def kernel(
    nb, nn, cap,
    vec_ref, cen_ref, owner_ref, local_ref,
    sums_ref, counts_ref, posted_ref,
    v_all, cen, cen_t, vec_t, norms, logit, prob, stats, mine, parts, got, total, place, box, acc,
    local_sem, v_send, v_recv, s_send, s_recv, m_send, m_recv, a_send, a_recv, o_sem,
):
    b = lax.axis_index("blk")
    n = lax.axis_index("narrow")
    before, after = lax.rem(b + nb - 1, nb), lax.rem(b + 1, nb)
    rows, width = vec_ref.shape
    cents = cen.shape[0]
    tile = min(512, cents)
    tiles = cents // tile

    def remote(src, dst, send, recv, blk, narrow):
        return pltpu.make_async_remote_copy(
            src_ref=src, dst_ref=dst, send_sem=send, recv_sem=recv,
            device_id={"blk": blk, "narrow": narrow}, device_id_type=MESH,
        )

    own_rows = pltpu.make_async_copy(vec_ref, v_all.at[n], local_sem.at[0])
    own_rows.start()
    own_cents = pltpu.make_async_copy(
        cen_ref.at[pl.ds(pl.multiple_of(n * cents, 16), cents)], cen, local_sem.at[1]
    )
    own_cents.start()

    barrier = pltpu.get_barrier_semaphore()

    def greet(blk, narrow):
        pl.semaphore_signal(
            barrier, inc=1, device_id={"blk": blk, "narrow": narrow}, device_id_type=MESH
        )

    for j in range(1, nn):
        other = lax.rem(n + j, nn)
        for blk in (b, before, after):
            greet(blk, other)

    @pl.loop(1, nb)
    def _(i):
        greet(lax.rem(b + i, nb), n)

    pl.semaphore_wait(barrier, 3 * (nn - 1) + nb - 1)

    def v_copy(j, back):
        other = lax.rem(n + j, nn)
        slot = n + nn * back
        at = j + nn * back
        return remote(
            vec_ref, v_all.at[slot], v_send.at[at], v_recv.at[slot], before if back else b, other
        )

    for j in range(nn):
        v_copy(j, 1).start()
        if j:
            v_copy(j, 0).start()

    own_cents.wait()
    for t in range(tiles):
        at = pl.ds(t * tile, tile)
        block = cen[at, :]
        wide = block.astype(F32)
        norms[at, :] = jnp.sum(wide * wide, axis=1, keepdims=True)
        cen_t[:, at] = block.T
    own_rows.wait()
    vec_t[...] = v_all[n].T

    up = lax.broadcasted_iota(jnp.int32, (rows, rows), 0)
    across = lax.broadcasted_iota(jnp.int32, (rows, rows), 1)
    owner_col = owner_ref[...].astype(F32)
    local_row = local_ref[...].astype(F32)
    owner_row = jnp.sum(jnp.where(up == across, owner_col, 0.0), axis=0, keepdims=True)
    local_col = jnp.sum(jnp.where(up == across, local_row, 0.0), axis=1, keepdims=True)
    ahead = (local_col < local_row) | ((local_col == local_row) & (up < across))
    rank = jnp.sum(
        jnp.where((owner_col == owner_row) & ahead, 1.0, 0.0), axis=0, keepdims=True
    )
    goes_to = owner_row * float(cap) + rank
    slots = lax.broadcasted_iota(jnp.int32, (nb * cap, rows), 0).astype(F32)
    place[...] = jnp.where(slots == goes_to, 1.0, 0.0).astype(BF16)

    def attend(step):
        far = step // nn
        k = lax.rem(n + step, nn)
        slot = k + nn * far
        vecs = v_all[slot]
        top = None
        for t in range(tiles):
            at = pl.ds(t * tile, tile)
            product = lax.dot_general(
                cen[at, :], vecs, (((1,), (1,)), ((), ())), preferred_element_type=F32
            )
            scores = 2.0 * product - norms[at, :]
            logit[slot, at, :] = scores
            high = jnp.max(scores, axis=0, keepdims=True)
            top = high if top is None else jnp.maximum(top, high)
        weight = None
        for t in range(tiles):
            at = pl.ds(t * tile, tile)
            p = jnp.exp(logit[slot, at, :] - top)
            prob[at, :] = p.astype(BF16)
            low = jnp.sum(p, axis=0, keepdims=True)
            weight = low if weight is None else weight + low
        first = lax.broadcasted_iota(jnp.int32, (8, rows), 0) < 4
        stats[far, n + nn * far, k] = jnp.where(first, top, weight)
        return far, k, slot, jnp.dot(cen_t[...], prob[...], preferred_element_type=F32)

    def m_copy(step):
        far = step // nn
        k = lax.rem(n + step, nn)
        slot = n + nn * far
        return remote(
            parts.at[step], got.at[slot], m_send.at[step], m_recv.at[slot],
            lax.rem(b + far, nb), k,
        )

    def s_copies(far):
        me = n + nn * far
        copies = []
        for j in range(nn):
            other = lax.rem(n + j, nn)
            if far:
                targets = [(after, 0, n + nn)] + ([(b, 1, n + nn)] if j else [])
            else:
                targets = ([(b, 0, n)] if j else []) + [(before, 1, n)]
            for i, (blk, group, where) in enumerate(targets):
                at = 2 * j + i
                copies.append(remote(
                    stats.at[far, me], stats.at[group, where], s_send.at[far, at],
                    s_recv.at[group, where], blk, other,
                ))
        return copies

    def attend_and_send(step):
        slot = lax.rem(n + step, nn) + nn * (step // nn)
        remote(
            vec_ref, v_all.at[slot], v_send.at[0], v_recv.at[slot], before, n
        ).wait_recv()
        mixed = attend(step)[3]
        parts[step] = mixed.astype(BF16)
        m_copy(step).start()

    mine[...] = attend(0)[3]

    @pl.loop(1, nn)
    def _(step):
        attend_and_send(step)

    for copy in s_copies(0):
        copy.start()

    @pl.loop(nn, 2 * nn)
    def _(step):
        attend_and_send(step)

    for copy in s_copies(1):
        copy.start()

    for group in range(2):
        me = n + nn * group

        @pl.loop(1, 2 * nn)
        def _(i, group=group, me=me):
            where = lax.rem(me + i, 2 * nn)
            remote(
                stats.at[group, where], stats.at[group, where], s_send.at[0, 0],
                s_recv.at[group, where], before, n,
            ).wait_recv()

    for group in range(2):
        for k in range(nn):
            tops = [stats[group, i, k][0:1, :] for i in range(2 * nn)]
            lows = [stats[group, i, k][4:5, :] for i in range(2 * nn)]
            top = functools.reduce(jnp.maximum, tops)
            mass = sum(low * jnp.exp(t - top) for t, low in zip(tops, lows))
            total[group * nn + k] = jnp.broadcast_to(top + jnp.log(mass), (8, rows))

    step_rows = cents // 8

    def o_copy(t):
        at = pl.ds(pl.multiple_of(t * step_rows, 16), step_rows)
        return pltpu.make_async_copy(acc.at[at], sums_ref.at[at], o_sem.at[t])

    def sum_up(t):
        at = pl.ds(pl.multiple_of(t * step_rows, 16), step_rows)
        weights = jnp.concatenate(
            [jnp.exp(logit[k, at, :] - total[k][0:1, :]).astype(BF16) for k in range(2 * nn)],
            axis=1,
        )
        acc[at, :] = jnp.dot(
            weights, v_all[...].reshape(2 * nn * rows, width), preferred_element_type=F32
        )
        tally = lax.dot_general(
            jnp.ones((8, 2 * nn * rows), BF16), weights, (((1,), (1,)), ((), ())),
            preferred_element_type=F32,
        )
        counts_ref[pl.ds(t, 1)] = tally[None, 0:1, :]
        o_copy(t).start()

    @pl.loop(0, EARLY)
    def _(t):
        sum_up(t)

    own_total = total[n][0:1, :]
    mine[...] = mine[...] * jnp.exp(stats[0, n, n][0:1, :] - own_total)

    @pl.loop(1, 2 * nn)
    def _(i):
        where = lax.rem(n + i, 2 * nn)
        remote(
            got.at[where], got.at[where], m_send.at[0], m_recv.at[where], before, n
        ).wait_recv()
        mine[...] += got[where].astype(F32) * jnp.exp(stats[0, where, n][0:1, :] - own_total)

    residual = (vec_t[...].astype(F32) - mine[...]).astype(BF16)
    box[...] = lax.dot_general(
        place[...], residual, (((1,), (1,)), ((), ())), preferred_element_type=F32
    ).astype(BF16)

    def block_of(i):
        return pl.ds(pl.multiple_of(i * cap, 16), cap)

    def a_copy(i):
        to = lax.rem(b + i, nb)
        return remote(
            box.at[block_of(to)], posted_ref.at[block_of(b)], a_send.at[i], a_recv.at[b], to, n
        )

    @pl.loop(1, nb)
    def _(i):
        a_copy(i).start()

    kept = pltpu.make_async_copy(
        box.at[block_of(b)], posted_ref.at[block_of(b)], local_sem.at[2]
    )
    kept.start()

    @pl.loop(EARLY, 8)
    def _(t):
        sum_up(t)

    @pl.loop(0, 8)
    def _(t):
        o_copy(t).wait()

    kept.wait()
    for j in range(nn):
        v_copy(j, 1).wait_send()
        if j:
            v_copy(j, 0).wait_send()
    for far in range(2):
        for copy in s_copies(far):
            copy.wait_send()

    @pl.loop(1, 2 * nn)
    def _(step):
        m_copy(step).wait_send()

    @pl.loop(1, nb)
    def _(i):
        source = lax.rem(b + i, nb)
        a_copy(i).wait_send()
        remote(
            box.at[block_of(source)], posted_ref.at[block_of(source)], a_send.at[i],
            a_recv.at[source], source, n,
        ).wait_recv()


def body(vectors, centroids, list_owner, list_local):
    nb, nn = lax.axis_size("blk"), lax.axis_size("narrow")
    rows, width = vectors.shape
    cents = centroids.shape[0] // nn
    cap = max(2, 2 * rows // nb)
    vmem = pl.BlockSpec(memory_space=pltpu.VMEM)
    hbm = pl.BlockSpec(memory_space=pl.ANY)
    dma = pltpu.SemaphoreType.DMA
    sums, counts, posted = pl.pallas_call(
        functools.partial(kernel, nb, nn, cap),
        out_shape=(
            jax.ShapeDtypeStruct((cents, width), F32),
            jax.ShapeDtypeStruct((8, 1, cents // 8), F32),
            jax.ShapeDtypeStruct((nb * cap, width), BF16),
        ),
        in_specs=[hbm, hbm, vmem, vmem],
        out_specs=(hbm, vmem, hbm),
        scratch_shapes=[
            pltpu.VMEM((2 * nn, rows, width), BF16),
            pltpu.VMEM((cents, width), BF16),
            pltpu.VMEM((width, cents), BF16),
            pltpu.VMEM((width, rows), BF16),
            pltpu.VMEM((cents, 1), F32),
            pltpu.VMEM((2 * nn, cents, rows), F32),
            pltpu.VMEM((cents, rows), BF16),
            pltpu.VMEM((2, 2 * nn, nn, 8, rows), F32),
            pltpu.VMEM((width, rows), F32),
            pltpu.VMEM((2 * nn, width, rows), BF16),
            pltpu.VMEM((2 * nn, width, rows), BF16),
            pltpu.VMEM((2 * nn, 8, rows), F32),
            pltpu.VMEM((nb * cap, rows), BF16),
            pltpu.VMEM((nb * cap, width), BF16),
            pltpu.VMEM((cents, width), F32),
            dma((3,)),
            dma((2 * nn,)),
            dma((2 * nn,)),
            dma((2, 2 * nn)),
            dma((2, 2 * nn)),
            dma((2 * nn,)),
            dma((2 * nn,)),
            dma((nb,)),
            dma((nb,)),
            dma((8,)),
        ],
        compiler_params=pltpu.CompilerParams(
            collective_id=0, has_side_effects=True, vmem_limit_bytes=56 * 1024 * 1024
        ),
        cost_estimate=pl.CostEstimate(
            flops=6 * 2 * nn * rows * cents * width, bytes_accessed=20 * cents * width,
            transcendentals=4 * nn * rows * cents,
        ),
    )(vectors, centroids, list_owner, list_local.reshape(1, rows))
    return sums, counts.reshape(cents), posted


def solution(mesh):
    in_specs = (
        P(("blk", "narrow"), None),
        P("blk", None),
        P(("blk", "narrow"), None),
        P(("blk", "narrow")),
    )
    out_specs = (P(("blk", "narrow"), None), P(("blk", "narrow")), P(("blk", "narrow"), None))
    return jax.shard_map(body, mesh=mesh, in_specs=in_specs, out_specs=out_specs, check_vma=False)
```

```python
import functools

import jax
import jax.numpy as jnp
from jax import lax
from jax.experimental import pallas as pl
from jax.experimental.pallas import tpu as pltpu
from jax.sharding import PartitionSpec as P

MESH = pl.DeviceIdType.MESH
F32 = jnp.float32
BF16 = jnp.bfloat16
PIECES = 2


def kernel(
    nb, nn, cap,
    vec_ref, cen_ref, owner_ref, local_ref,
    sums_ref, counts_ref, posted_ref,
    v_all, cen, cen_t, vec_t, norms, logit, prob, stats, mine, parts, got, total, place, box, acc,
    local_sem, v_send, v_recv, s_send, s_recv, m_send, m_recv, a_send, a_recv, o_sem,
):
    b = lax.axis_index("blk")
    n = lax.axis_index("narrow")
    before, after = lax.rem(b + nb - 1, nb), lax.rem(b + 1, nb)
    rows, width = vec_ref.shape
    cents = cen.shape[0]
    tile = min(512, cents)
    tiles = cents // tile

    def remote(src, dst, send, recv, blk, narrow):
        return pltpu.make_async_remote_copy(
            src_ref=src, dst_ref=dst, send_sem=send, recv_sem=recv,
            device_id={"blk": blk, "narrow": narrow}, device_id_type=MESH,
        )

    own_rows = pltpu.make_async_copy(vec_ref, v_all.at[n], local_sem.at[0])
    own_rows.start()
    own_cents = pltpu.make_async_copy(
        cen_ref.at[pl.ds(pl.multiple_of(n * cents, 16), cents)], cen, local_sem.at[1]
    )
    own_cents.start()

    barrier = pltpu.get_barrier_semaphore()

    def greet(blk, narrow):
        pl.semaphore_signal(
            barrier, inc=1, device_id={"blk": blk, "narrow": narrow}, device_id_type=MESH
        )

    for j in range(1, nn):
        other = lax.rem(n + j, nn)
        for blk in (b, before, after):
            greet(blk, other)

    @pl.loop(1, nb)
    def _(i):
        greet(lax.rem(b + i, nb), n)

    pl.semaphore_wait(barrier, 3 * (nn - 1) + nb - 1)

    def near_copy(j):
        return remote(
            vec_ref, v_all.at[n], v_send.at[j], v_recv.at[n], b, lax.rem(n + j, nn)
        )

    def far_copy(step):
        k = lax.rem(n + step, nn)
        source = vec_ref if isinstance(step, int) else v_all.at[k]
        return remote(
            source, v_all.at[nn + k], v_send.at[nn + step], v_recv.at[nn + k], before, n
        )

    for j in range(1, nn):
        near_copy(j).start()
    far_copy(0).start()

    own_cents.wait()
    for t in range(tiles):
        at = pl.ds(t * tile, tile)
        block = cen[at, :]
        wide = block.astype(F32)
        norms[at, :] = jnp.sum(wide * wide, axis=1, keepdims=True)
        cen_t[:, at] = block.T
    own_rows.wait()
    vec_t[...] = v_all[n].T

    up = lax.broadcasted_iota(jnp.int32, (rows, rows), 0)
    across = lax.broadcasted_iota(jnp.int32, (rows, rows), 1)
    owner_row = owner_ref[...].astype(F32)
    local_row = local_ref[...].astype(F32)
    owner_col = jnp.sum(jnp.where(up == across, owner_row, 0.0), axis=1, keepdims=True)
    local_col = jnp.sum(jnp.where(up == across, local_row, 0.0), axis=1, keepdims=True)
    ahead = (local_col < local_row) | ((local_col == local_row) & (up < across))
    rank = jnp.sum(
        jnp.where((owner_col == owner_row) & ahead, 1.0, 0.0), axis=0, keepdims=True
    )
    goes_to = owner_row * float(cap) + rank
    slots = lax.broadcasted_iota(jnp.int32, (nb * cap, rows), 0).astype(F32)
    place[...] = jnp.where(slots == goes_to, 1.0, 0.0).astype(BF16)

    def attend(step):
        far = step // nn
        k = lax.rem(n + step, nn)
        slot = k + nn * far
        vecs = v_all[slot]
        top = None
        for t in range(tiles):
            at = pl.ds(t * tile, tile)
            product = lax.dot_general(
                cen[at, :], vecs, (((1,), (1,)), ((), ())), preferred_element_type=F32
            )
            scores = 2.0 * product - norms[at, :]
            logit[slot, at, :] = scores
            high = jnp.max(scores, axis=0, keepdims=True)
            top = high if top is None else jnp.maximum(top, high)
        weight = None
        for t in range(tiles):
            at = pl.ds(t * tile, tile)
            p = jnp.exp(logit[slot, at, :] - top)
            prob[at, :] = p.astype(BF16)
            low = jnp.sum(p, axis=0, keepdims=True)
            weight = low if weight is None else weight + low
        first = lax.broadcasted_iota(jnp.int32, (8, rows), 0) < 4
        stats[far, n + nn * far, k] = jnp.where(first, top, weight)
        return far, k, slot, jnp.dot(cen_t[...], prob[...], preferred_element_type=F32)

    part = width // PIECES

    def m_copy(step, piece):
        far = step // nn
        k = lax.rem(n + step, nn)
        slot = n + nn * far
        at = pl.ds(piece * part, part)
        return remote(
            parts.at[step, at], got.at[slot, at], m_send.at[piece, step],
            m_recv.at[piece, slot], lax.rem(b + far, nb), k,
        )

    def s_copies(far):
        me = n + nn * far
        copies = []
        for j in range(nn):
            other = lax.rem(n + j, nn)
            if far:
                targets = [(after, 0, n + nn)] + ([(b, 1, n + nn)] if j else [])
            else:
                targets = ([(b, 0, n)] if j else []) + [(before, 1, n)]
            for i, (blk, group, where) in enumerate(targets):
                at = 2 * j + i
                copies.append(remote(
                    stats.at[far, me], stats.at[group, where], s_send.at[far, at],
                    s_recv.at[group, where], blk, other,
                ))
        return copies

    def wait_rows(step):
        slot = lax.rem(n + step, nn) + nn * (step // nn)
        remote(
            vec_ref, v_all.at[slot], v_send.at[0], v_recv.at[slot], before, n
        ).wait_recv()

    mine[...] = attend(0)[3]

    @pl.loop(1, nn)
    def _(step):
        wait_rows(step)
        far_copy(step).start()
        parts[step] = attend(step)[3].astype(BF16)
        for piece in range(PIECES):
            m_copy(step, piece).start()

    for copy in s_copies(0):
        copy.start()

    @pl.loop(nn, 2 * nn)
    def _(step):
        wait_rows(step)
        parts[step] = attend(step)[3].astype(BF16)
        m_copy(step, 0).start()

    for copy in s_copies(1):
        copy.start()

    @pl.loop(nn, 2 * nn)
    def _(step):
        for piece in range(1, PIECES):
            m_copy(step, piece).start()

    for group in range(2):
        me = n + nn * group

        @pl.loop(1, 2 * nn)
        def _(i, group=group, me=me):
            where = lax.rem(me + i, 2 * nn)
            remote(
                stats.at[group, where], stats.at[group, where], s_send.at[0, 0],
                s_recv.at[group, where], before, n,
            ).wait_recv()

    for group in range(2):
        for k in range(nn):
            tops = [stats[group, i, k][0:1, :] for i in range(2 * nn)]
            lows = [stats[group, i, k][4:5, :] for i in range(2 * nn)]
            top = functools.reduce(jnp.maximum, tops)
            mass = sum(low * jnp.exp(t - top) for t, low in zip(tops, lows))
            total[group * nn + k] = jnp.broadcast_to(top + jnp.log(mass), (8, rows))

    step_rows = cents // 8

    def o_copy(t):
        at = pl.ds(pl.multiple_of(t * step_rows, 16), step_rows)
        return pltpu.make_async_copy(acc.at[at], sums_ref.at[at], o_sem.at[t])

    def sum_up(t):
        at = pl.ds(pl.multiple_of(t * step_rows, 16), step_rows)
        weights = jnp.concatenate(
            [jnp.exp(logit[k, at, :] - total[k][0:1, :]).astype(BF16) for k in range(2 * nn)],
            axis=1,
        )
        acc[at, :] = jnp.dot(
            weights, v_all[...].reshape(2 * nn * rows, width), preferred_element_type=F32
        )
        tally = lax.dot_general(
            jnp.ones((8, 2 * nn * rows), BF16), weights, (((1,), (1,)), ((), ())),
            preferred_element_type=F32,
        )
        counts_ref[pl.ds(t, 1)] = tally[None, 0:1, :]
        o_copy(t).start()

    def block_of(i):
        return pl.ds(pl.multiple_of(i * cap, 16), cap)

    def a_copy(i, piece):
        to = lax.rem(b + i, nb)
        at = pl.ds(piece * part, part)
        return remote(
            box.at[block_of(to), at], posted_ref.at[block_of(b), at], a_send.at[piece, i],
            a_recv.at[piece, b], to, n,
        )

    own_total = total[n][0:1, :]
    own_share = jnp.exp(stats[0, n, n][0:1, :] - own_total)
    for piece in range(PIECES):
        at = pl.ds(piece * part, part)
        mine[at, :] = mine[at, :] * own_share

        @pl.loop(1, 2 * nn)
        def _(i, piece=piece, at=at):
            where = lax.rem(n + i, 2 * nn)
            remote(
                got.at[where, at], got.at[where, at], m_send.at[0, 0],
                m_recv.at[piece, where], before, n,
            ).wait_recv()
            share = jnp.exp(stats[0, where, n][0:1, :] - own_total)
            mine[at, :] += got[where, at, :].astype(F32) * share

        residual = (vec_t[at, :].astype(F32) - mine[at, :]).astype(BF16)
        box[:, at] = lax.dot_general(
            place[...], residual, (((1,), (1,)), ((), ())), preferred_element_type=F32
        ).astype(BF16)

        @pl.loop(1, nb)
        def _(i, piece=piece):
            a_copy(i, piece).start()

    kept = pltpu.make_async_copy(
        box.at[block_of(b)], posted_ref.at[block_of(b)], local_sem.at[2]
    )
    kept.start()

    @pl.loop(0, 8)
    def _(t):
        sum_up(t)

    @pl.loop(0, 8)
    def _(t):
        o_copy(t).wait()

    kept.wait()
    far_copy(0).wait_send()
    for far in range(2):
        for copy in s_copies(far):
            copy.wait_send()

    @pl.loop(1, nn)
    def _(step):
        near_copy(step).wait_send()
        far_copy(step).wait_send()

    for piece in range(PIECES):
        at = pl.ds(piece * part, part)

        @pl.loop(1, 2 * nn)
        def _(step, piece=piece):
            m_copy(step, piece).wait_send()

        @pl.loop(1, nb)
        def _(i, piece=piece, at=at):
            source = lax.rem(b + i, nb)
            a_copy(i, piece).wait_send()
            remote(
                box.at[block_of(source), at], posted_ref.at[block_of(source), at],
                a_send.at[piece, i], a_recv.at[piece, source], source, n,
            ).wait_recv()


def body(vectors, centroids, list_owner, list_local):
    nb, nn = lax.axis_size("blk"), lax.axis_size("narrow")
    rows, width = vectors.shape
    cents = centroids.shape[0] // nn
    cap = max(2, 2 * rows // nb)
    vmem = pl.BlockSpec(memory_space=pltpu.VMEM)
    hbm = pl.BlockSpec(memory_space=pl.ANY)
    dma = pltpu.SemaphoreType.DMA
    sums, counts, posted = pl.pallas_call(
        functools.partial(kernel, nb, nn, cap),
        out_shape=(
            jax.ShapeDtypeStruct((cents, width), F32),
            jax.ShapeDtypeStruct((8, 1, cents // 8), F32),
            jax.ShapeDtypeStruct((nb * cap, width), BF16),
        ),
        in_specs=[hbm, hbm, vmem, vmem],
        out_specs=(hbm, vmem, hbm),
        scratch_shapes=[
            pltpu.VMEM((2 * nn, rows, width), BF16),
            pltpu.VMEM((cents, width), BF16),
            pltpu.VMEM((width, cents), BF16),
            pltpu.VMEM((width, rows), BF16),
            pltpu.VMEM((cents, 1), F32),
            pltpu.VMEM((2 * nn, cents, rows), F32),
            pltpu.VMEM((cents, rows), BF16),
            pltpu.VMEM((2, 2 * nn, nn, 8, rows), F32),
            pltpu.VMEM((width, rows), F32),
            pltpu.VMEM((2 * nn, width, rows), BF16),
            pltpu.VMEM((2 * nn, width, rows), BF16),
            pltpu.VMEM((2 * nn, 8, rows), F32),
            pltpu.VMEM((nb * cap, rows), BF16),
            pltpu.VMEM((nb * cap, width), BF16),
            pltpu.VMEM((cents, width), F32),
            dma((3,)),
            dma((2 * nn,)),
            dma((2 * nn,)),
            dma((2, 2 * nn)),
            dma((2, 2 * nn)),
            dma((PIECES, 2 * nn)),
            dma((PIECES, 2 * nn)),
            dma((PIECES, nb)),
            dma((PIECES, nb)),
            dma((8,)),
        ],
        compiler_params=pltpu.CompilerParams(
            collective_id=0, has_side_effects=True, vmem_limit_bytes=56 * 1024 * 1024
        ),
        cost_estimate=pl.CostEstimate(
            flops=6 * 2 * nn * rows * cents * width, bytes_accessed=20 * cents * width,
            transcendentals=4 * nn * rows * cents,
        ),
    )(vectors, centroids, list_owner.reshape(1, rows), list_local.reshape(1, rows))
    return sums, counts.reshape(cents), posted


def solution(mesh):
    in_specs = (
        P(("blk", "narrow"), None),
        P("blk", None),
        P(("blk", "narrow"), None),
        P(("blk", "narrow")),
    )
    out_specs = (P(("blk", "narrow"), None), P(("blk", "narrow")), P(("blk", "narrow"), None))
    return jax.shard_map(body, mesh=mesh, in_specs=in_specs, out_specs=out_specs, check_vma=False)
```
